32 devices in a mesh: seq: 4 (over y, x), head: 8 (over z, core).
Axes of the slice: x: 2, y: 2, z: 4, core: 2. Of those that a mesh axis runs over, the one named last changes fastest.
Arguments:
- tokens: bfloat16 [2048, 2048], P('seq'), may hold values from -40 to 40
- attention_gain: float32 [2048], replicated, may hold values from 0.1 to 1.9
- head_weights: bfloat16 [3, 2048, 2048], P(None, None, 'head'), may hold values from -1 to 1
- carried_state: float32 [8256, 2048], P(None, 'head'), may hold values from -384 to 384
- output_weight: bfloat16 [2048, 2048], P('head'), may hold values from -0.125 to 0.125
- expert_gain: float32 [2048], replicated, may hold values from 0.1 to 1.9
- router_weight: bfloat16 [2048, 64], replicated, may hold values from -0.125 to 0.125
- expert_index: int32 [2048, 8], P(('seq', 'head')), may hold values from 0 to 63, all different within a row; in each aligned block of 64 rows (0 to 63, 64 to 127, ...) at most 12 rows name the same one
- expert_first: bfloat16 [2, 2048, 65536], P(None, None, ('seq', 'head')), may hold values from -0.125 to 0.125
- expert_second: bfloat16 [65536, 2048], P(('seq', 'head')), may hold values from -0.1875 to 0.1875
Outputs:
- layer_out: bfloat16 [2048, 2048], P(('seq', 'head'))
The draws below stay inside these ranges and needn't reach their ends.
Inputs may be any that keep to these rules, and one draw needn't show every extreme that they name: `expert_index`: each row names 8 different experts; within each aligned block of 64 rows (the rows of one device) no expert is named by more than 12 rows.
All inputs are finite; a program needn't handle non-finite values.
Results may differ from the reference program's by a relative error of at most 0.019.
Values may be sent and summed in bfloat16 or wider, within the bound.
A program may use at most 192 MiB of HBM per device.

```python
import math
import jax
import jax.numpy as jnp
import numpy as np
from jax import lax

HD = 128
HEADS = 16
D = 2048
STATE = 8256
EXPERTS = 64
TOP = 8
FF = 1024
TOK_SEQ = 512
TOKENS = 2048
SLAB = 64
CAP = 12
SPLIT = 1
N_SEQ = 4


def draw_tokens(key, part):
    key = jax.random.fold_in(key, 11)
    jitter_key, row_key, column_key = jax.random.split(key, 3)
    jitter = jax.random.truncated_normal(jitter_key, -4.0, 4.0, (TOKENS, D), jnp.float32)
    row_scale = jnp.exp(jax.random.uniform(row_key, (TOKENS, 1), jnp.float32, math.log(0.3), math.log(3.0)))
    column_scale = jnp.exp(jax.random.uniform(column_key, (1, D), jnp.float32, -0.5 * math.log(10.0), 0.5 * math.log(10.0)))
    return (row_scale * (jitter * column_scale)).astype(jnp.bfloat16)


def draw_head_weights(key, part):
    key = jax.random.fold_in(key, 23)
    entry_key, column_key = jax.random.split(key)
    entries = jax.random.truncated_normal(entry_key, -4.0, 4.0, (3, D, D), jnp.float32)
    column_scale = jnp.exp(jax.random.uniform(column_key, (3, 1, D), jnp.float32, -0.5 * math.log(10.0), 0.5 * math.log(10.0)))
    return (entries * column_scale / math.sqrt(D)).astype(jnp.bfloat16)


def level_of(key, extent, cuts, least, high):
    level = 1.0
    for position, blocks in cuts:
        draws = jax.random.uniform(jax.random.fold_in(jax.random.fold_in(key, 6), position), (blocks,), jnp.float32, least / len(cuts), high / len(cuts))
        level = level * jnp.repeat(jnp.exp(draws), extent[position] // blocks).reshape((-1,) + (1,) * (len(extent) - 1 - position))
    return level


def shared_out(own_key, own, number, rows, number_of, top, most, lean):
    order = jax.random.permutation(own_key, number_of)
    crowded, usual = load_shares(number_of, rows * top, most, lean, True), load_shares(number_of, rows * top, most, lean, False)
    places = jnp.arange(number_of)

    def named(sizes, rotation):
        used = int((sizes > 0).sum())
        fixed = max(1, used // 4)
        passed = fixed + (places - fixed + rotation * (used - fixed)) % max(1, number_of - fixed)
        return jnp.zeros((number_of,), jnp.int32).at[order[jnp.where(places < fixed, places, passed)]].set(jnp.asarray(sizes, jnp.int32))

    sizes = jnp.where(number % 4 == 0, named(crowded, number // 4), named(usual, number - number // 4 - 1))
    mixed = jax.random.permutation(jax.random.fold_in(own, 3), number_of)
    source_of, receiver = mixed[0:number_of // 2 * 2:2], mixed[1:number_of // 2 * 2:2]
    margin = jnp.minimum(sizes[source_of] - 1, most - sizes[receiver]) // 2
    margin = jnp.where((source_of == order[0]) | (receiver == order[0]) | (sizes[receiver] == 0), 0, jnp.maximum(margin, 0))
    passed = jax.random.randint(jax.random.fold_in(own, 4), (number_of // 2,), 0, 1 << 20) % (margin + 1)
    sizes = sizes.at[source_of].add(-passed).at[receiver].add(passed)
    members = jnp.searchsorted(jnp.cumsum(sizes), jnp.arange(rows * top), side="right").astype(jnp.int32)
    grid = members.reshape(top, rows).T
    grid = grid[jax.random.permutation(jax.random.fold_in(own, 1), rows)]
    rotation = jax.random.randint(jax.random.fold_in(own, 2), (rows, 1), 0, top)
    return jnp.take_along_axis(grid, (jnp.arange(top)[None, :] + rotation) % top, axis=1)


def load_shares(count, total, most, skew, full):
    loads = [(1 << 20) // math.isqrt(grade ** skew) + 1 for grade in range(1, count + 1)]
    largest = most if full else min(most, max(-(-total // count), total * loads[0] // sum(loads)))
    least = 1 if total - largest >= count - 1 else 0
    counts, spare = [largest] + [least] * (count - 1), total - largest - least * (count - 1)
    while spare > 0:
        movable = [i for i in range(1, count) if counts[i] < largest] or [i for i in range(1, count) if counts[i] < most]
        pool, left = sum([loads[i] for i in movable]), spare
        for i in movable:
            extra = min(most - counts[i], max(1, left * loads[i] // pool), spare)
            counts[i] = counts[i] + extra
            spare = spare - extra
    return np.array(counts)


def normal_values(key, dims, scale, bound, cuts=(), kind=jnp.bfloat16):
    drawn = jax.random.normal(key, dims, jnp.float32) * scale
    if len(cuts) > 0:
        drawn = level_of(key, dims, cuts, -0.22, 0.18) * drawn
    return jnp.clip(drawn, min=-bound, max=bound).astype(kind)


def setup_inputs(seed: int = 0) -> dict:
    key_list = jax.random.split(jax.random.key(seed), 11)
    tokens = draw_tokens(jax.random.fold_in(key_list[10], 71), 0)
    attention_gain = jnp.clip(1.0 + 0.18 * jax.random.normal(key_list[1], (D,), jnp.float32), 0.1, 1.9)
    head_weights = draw_head_weights(jax.random.fold_in(key_list[10], 71), 0)
    carried_state = normal_values(key_list[3], (STATE, D), 64.0, 384.0, ((1, 8),), jnp.float32)
    output_weight = normal_values(key_list[4], (D, D), D ** -0.5, 0.125, ((0, 8),))
    expert_gain = jnp.clip(1.0 + 0.18 * jax.random.normal(key_list[5], (D,), jnp.float32), 0.1, 1.9)
    router_weight = normal_values(key_list[6], (D, EXPERTS), D ** -0.5, 0.125)
    expert_index_keys = jax.random.split(jax.random.fold_in(key_list[7], 1), TOKENS // SLAB)
    expert_index_turns = jax.random.permutation(jax.random.fold_in(key_list[7], 3), TOKENS // SLAB)
    expert_index = jax.vmap(lambda own, number: shared_out(jax.random.fold_in(key_list[7], 2), own, number, SLAB, EXPERTS, TOP, CAP, 2))(expert_index_keys, expert_index_turns).reshape((TOKENS, TOP))
    expert_first = normal_values(key_list[8], (2, D, EXPERTS * FF), D ** -0.5, 0.125, ((2, 32),))
    expert_second = normal_values(key_list[9], (EXPERTS * FF, D), FF ** -0.5, 0.1875, ((0, 32),))
    return dict(tokens=tokens, attention_gain=attention_gain, head_weights=head_weights, carried_state=carried_state, output_weight=output_weight, expert_gain=expert_gain, router_weight=router_weight, expert_index=expert_index, expert_first=expert_first, expert_second=expert_second)


def features(vectors):
    breadth = vectors.shape[1]
    pieces = []
    for column in range(breadth):
        factors = np.concatenate([np.ones((1,), np.float32), np.full((breadth - column - 1,), math.sqrt(2.0), np.float32)])
        pieces.append(vectors[:, column:column + 1] * (vectors[:, column:] * factors))
    return jnp.concatenate(pieces, axis=1)

def norm_scaled(values, gain):
    return values * lax.rsqrt(lax.optimization_barrier(jnp.mean(values * values, axis=-1, keepdims=True)) + 1e-06) * gain

def head_output(operands):
    query_rows, key_rows, value_rows, memory = operands
    value_float = value_rows.astype(jnp.float32)
    key_place = jnp.arange(TOKENS, dtype=jnp.int32)

    def block_output(block_num):
        offset = (block_num * TOK_SEQ).astype(jnp.int32)
        query_block = lax.dynamic_slice_in_dim(query_rows, offset, TOK_SEQ, 0)
        scores = lax.dot_general(query_block, key_rows, (((1,), (1,)), ((), ())), preferred_element_type=jnp.float32)
        query_place = offset + jnp.arange(TOK_SEQ, dtype=jnp.int32)
        weights = jnp.where(key_place[None, :] <= query_place[:, None], scores * scores, 0.0)
        nearby = jnp.dot(weights, value_float, precision=lax.Precision.HIGHEST)
        lifted = features(query_block.astype(jnp.float32))
        carried = jnp.dot(lifted, memory, precision=lax.Precision.HIGHEST)
        return (nearby + carried) / HD
    outputs = lax.map(block_output, jnp.arange(N_SEQ, dtype=jnp.int32))
    return outputs.reshape(TOKENS, HD)

def reference(tokens, attention_gain, head_weights, carried_state, output_weight, expert_gain, router_weight, expert_index, expert_first, expert_second):
    floats = tokens.astype(jnp.float32)
    normed = norm_scaled(floats, attention_gain).astype(jnp.bfloat16)
    query_rows = jnp.dot(normed, head_weights[0], preferred_element_type=jnp.float32).astype(jnp.bfloat16)
    key_rows = jnp.dot(normed, head_weights[1], preferred_element_type=jnp.float32).astype(jnp.bfloat16)
    value_rows = jnp.dot(normed, head_weights[2], preferred_element_type=jnp.float32).astype(jnp.bfloat16)

    def by_head(matrix):
        return matrix.reshape(TOKENS, HEADS, HD).transpose(1, 0, 2)
    memories = carried_state.reshape(STATE, HEADS, HD).transpose(1, 0, 2)
    raw_heads = lax.map(head_output, (by_head(query_rows), by_head(key_rows), by_head(value_rows), memories))
    attended = norm_scaled(raw_heads, 1.0).astype(jnp.bfloat16).transpose(1, 0, 2).reshape(TOKENS, D)
    residual = floats + jnp.dot(attended, output_weight, preferred_element_type=jnp.float32)
    expert_input = norm_scaled(residual, expert_gain).astype(jnp.bfloat16)
    logits = jnp.dot(expert_input, router_weight, preferred_element_type=jnp.float32)
    gate_values = jax.nn.sigmoid(jnp.take_along_axis(logits, expert_index, axis=1))
    flat_index = expert_index.reshape(TOKENS * TOP)
    flat_gates = gate_values.reshape(TOKENS * TOP)
    owners = (jnp.arange(TOKENS * TOP, dtype=jnp.int32) // TOP).astype(jnp.int32)
    capacity_rows = TOKENS // SLAB * CAP
    piece_width = FF // SPLIT

    def expert_step(running, expert):
        chosen = flat_index == expert
        places = (jnp.cumsum(chosen.astype(jnp.int32)) - 1).astype(jnp.int32)
        targets = jnp.where(chosen, places, capacity_rows).astype(jnp.int32)
        row_ids = jnp.zeros((capacity_rows,), jnp.int32).at[targets].set(owners, mode='drop')
        weights = jnp.zeros((capacity_rows,), jnp.float32).at[targets].set(flat_gates, mode='drop')
        inputs = jnp.take(expert_input, row_ids, axis=0)
        first_cols = lax.dynamic_slice_in_dim(expert_first, (expert * FF).astype(jnp.int32), FF, 2)
        gate_part = jnp.dot(inputs, first_cols[0], preferred_element_type=jnp.float32)
        up_part = jnp.dot(inputs, first_cols[1], preferred_element_type=jnp.float32)
        hidden = (jax.nn.silu(gate_part) * up_part).astype(jnp.bfloat16)
        outputs = jnp.zeros((capacity_rows, D), jnp.float32)
        for portion in range(SPLIT):
            down_rows = lax.dynamic_slice_in_dim(expert_second, (expert * FF + portion * piece_width).astype(jnp.int32), piece_width, 0)
            product = jnp.dot(hidden[:, portion * piece_width:(portion + 1) * piece_width], down_rows, preferred_element_type=jnp.float32)
            rounded = lax.optimization_barrier(product.astype(jnp.bfloat16))
            outputs = outputs + rounded.astype(jnp.float32)
        return (running.at[row_ids].add(weights[:, None] * outputs), None)
    expert_sum, unused = lax.scan(expert_step, jnp.zeros((TOKENS, D), jnp.float32), jnp.arange(EXPERTS, dtype=jnp.int32))
    return (residual + expert_sum).astype(jnp.bfloat16)
```

```python
import functools
import math

import jax
import jax.numpy as jnp
from jax import lax
from jax.experimental import pallas as pl
from jax.experimental.pallas import tpu as pltpu
from jax.sharding import PartitionSpec as P

HD = 128
EXPERTS = 64
TOP = 8


def partner_2(array, axis, apart):
    return lax.ppermute(array, axis, [(i, i ^ 1 << apart) for i in range(lax.axis_size(axis))])


def norm_scaled(values, gain):
    return values * lax.rsqrt(jnp.mean(values * values, axis=-1, keepdims=True) + 1e-06) * gain


def carried_kernel(breadth, heads, width, q_ref, memory_ref, out_ref, slab_ref):
    group = 16
    tokens = q_ref.shape[1]
    part = min(256, tokens)
    out_ref[...] = jnp.zeros_like(out_ref)
    place = lax.broadcasted_iota(jnp.int32, (breadth, heads * width), 0)

    def step(a, carry):
        for b in range(group):
            i = a * group + b
            fixed = (breadth - 1) * b - b * (b - 1) // 2
            shift = fixed % 8
            base = (
                a * (group * (breadth - 1) + group // 2)
                - a * a * (group * group // 2)
                - a * (group * b)
                + (fixed - shift)
            )
            rows = breadth + 8 if shift else breadth
            slab = memory_ref[pl.ds(pl.multiple_of(base, 8), rows), :]
            slab = slab[shift : shift + breadth]
            factor = jnp.where(place > i, math.sqrt(2.0), jnp.where(place == i, 1.0, 0.0))
            slab_ref[b] = (slab * factor).T.astype(jnp.bfloat16)
        for head in range(heads):
            q_rows = q_ref[pl.ds(pl.multiple_of(head * breadth + a * group, group), group), :]
            for first in range(0, tokens, part):
                columns = slice(first, first + part)
                weights = q_ref[head * breadth : (head + 1) * breadth, columns].astype(jnp.bfloat16)
                total = out_ref[head * width : (head + 1) * width, columns]
                for b in range(group):
                    inner = jnp.dot(
                        slab_ref[b, head * width : (head + 1) * width, :],
                        weights,
                        preferred_element_type=jnp.float32,
                    )
                    total = total + inner * q_rows[b : b + 1, columns]
                out_ref[head * width : (head + 1) * width, columns] = total
        return carry

    lax.fori_loop(0, breadth // group, step, 0)


def apply_carried(q_t, memory, heads, width):
    tokens = q_t.shape[1]
    return pl.pallas_call(
        functools.partial(carried_kernel, HD, heads, width),
        out_shape=jax.ShapeDtypeStruct((heads * width, tokens), jnp.float32),
        in_specs=[pl.BlockSpec(memory_space=pltpu.VMEM)] * 2,
        out_specs=pl.BlockSpec(memory_space=pltpu.VMEM),
        scratch_shapes=[pltpu.VMEM((16, heads * width, HD), jnp.bfloat16)],
        compiler_params=pltpu.CompilerParams(vmem_limit_bytes=40 * 2**20),
        cost_estimate=pl.CostEstimate(
            flops=4 * heads * width * HD * HD * tokens,
            bytes_accessed=memory.size * 4,
            transcendentals=0,
        ),
        name="carried_state",
    )(q_t, memory)


def causal_kernel(heads, width, me_ref, q_ref, keys_ref, values_ref, carried_ref, out_ref):
    shards, rows, _ = keys_ref.shape
    tokens = q_ref.shape[1]
    mine = me_ref[0]
    key_place = lax.broadcasted_iota(jnp.int32, (rows, tokens), 0)
    query_place = lax.broadcasted_iota(jnp.int32, (rows, tokens), 1) + mine * rows
    out_ref[...] = carried_ref[...]

    def shard_step(shard, carry):
        visible = key_place + shard * rows <= query_place
        for head in range(heads):
            scores = jnp.dot(
                keys_ref[shard, :, head * HD : (head + 1) * HD],
                q_ref[head * HD : (head + 1) * HD, :].astype(jnp.bfloat16),
                preferred_element_type=jnp.float32,
            )
            weights = jnp.where(visible, scores * scores, 0.0).astype(jnp.bfloat16)
            out_ref[head * width : (head + 1) * width, :] += lax.dot_general(
                values_ref[shard, :, head * width : (head + 1) * width],
                weights,
                (((0,), (0,)), ((), ())),
                preferred_element_type=jnp.float32,
            )
        return carry

    lax.fori_loop(0, mine + 1, shard_step, 0)


def causal_rows(q_t, keys, values, carried, heads, width):
    return pl.pallas_call(
        functools.partial(causal_kernel, heads, width),
        out_shape=jax.ShapeDtypeStruct(carried.shape, jnp.float32),
        in_specs=[pl.BlockSpec(memory_space=pltpu.SMEM)]
        + [pl.BlockSpec(memory_space=pltpu.VMEM)] * 4,
        out_specs=pl.BlockSpec(memory_space=pltpu.VMEM),
        compiler_params=pltpu.CompilerParams(vmem_limit_bytes=40 * 2**20),
        name="causal_scores",
    )(lax.axis_index("seq").astype(jnp.int32).reshape(1), q_t, keys, values, carried)


def body(
    tokens,
    attention_gain,
    head_weights,
    carried_state,
    output_weight,
    expert_gain,
    router_weight,
    expert_index,
    expert_first,
    expert_second,
):
    shard_rows = tokens.shape[0]
    model_width = tokens.shape[1]
    floats = tokens.astype(jnp.float32)
    normed = norm_scaled(floats, attention_gain).astype(jnp.bfloat16)
    projected = jnp.einsum(
        "td,adc->atc", normed, head_weights, preferred_element_type=jnp.float32
    ).astype(jnp.bfloat16)
    query_rows, key_rows, value_rows = (projected[0], projected[1], projected[2])
    share = value_rows.shape[1]
    local_heads = max(1, share // HD)
    value_width = share // local_heads
    if value_width < HD:
        mine = jnp.stack([query_rows, key_rows])
        partner = partner_2(mine, "head", 0)
        lower = lax.axis_index("head") % 2 == 0
        joined = jnp.where(
            lower,
            jnp.concatenate([mine, partner], axis=2),
            jnp.concatenate([partner, mine], axis=2),
        )
        query_rows, key_rows = (joined[0], joined[1])

    gathered = lax.all_gather(jnp.concatenate([key_rows, value_rows], axis=1), "seq")
    key_width = key_rows.shape[1]
    q_t = query_rows.T.astype(jnp.float32)
    carried = apply_carried(q_t, carried_state, local_heads, value_width)
    raw_t = causal_rows(
        q_t,
        gathered[:, :, :key_width],
        gathered[:, :, key_width:],
        carried,
        local_heads,
        value_width,
    ).reshape(local_heads, value_width, shard_rows) / HD
    squares = jnp.sum(raw_t * raw_t, axis=1, keepdims=True)
    if value_width < HD:
        squares = squares + partner_2(squares, "head", 0)
    scaled_heads = (raw_t * lax.rsqrt(squares / HD + 1e-06)).astype(jnp.bfloat16)
    attended = scaled_heads.reshape(share, shard_rows).T
    slab_rows = expert_index.shape[0]
    attention_sum = lax.psum_scatter(
        jnp.dot(attended, output_weight, preferred_element_type=jnp.float32).astype(jnp.bfloat16),
        "head",
        scatter_dimension=0,
        tiled=True,
    ).astype(jnp.float32)
    token_slab = lax.dynamic_slice_in_dim(floats, lax.axis_index("head") * slab_rows, slab_rows, 0)
    residual = token_slab + attention_sum
    expert_input = norm_scaled(residual, expert_gain).astype(jnp.bfloat16)
    logits = jnp.dot(expert_input, router_weight, preferred_element_type=jnp.float32)
    matches = expert_index[:, :, None] == jnp.arange(EXPERTS, dtype=jnp.int32)
    gate_values = jax.nn.sigmoid(jnp.sum(jnp.where(matches, logits[:, None, :], 0.0), axis=2))
    flat_matches = matches.reshape(slab_rows * TOP, EXPERTS).astype(jnp.int32)
    earlier = jnp.cumsum(flat_matches, axis=0) - flat_matches
    slots = jnp.sum(earlier * flat_matches, axis=1).reshape(slab_rows, TOP)
    devices = lax.axis_size("seq") * lax.axis_size("head")
    piece_count = max(1, devices // EXPERTS)
    local_experts = max(1, EXPERTS // devices)
    capacity = max(2, 3 * slab_rows * TOP // (2 * EXPERTS))
    groups = EXPERTS * piece_count
    targets = (slots * groups + expert_index * piece_count)[:, :, None] + jnp.arange(
        piece_count, dtype=jnp.int32
    )
    send_map = jnp.sum(
        (
            targets.reshape(slab_rows, TOP * piece_count, 1)
            == jnp.arange(capacity * groups, dtype=jnp.int32)
        ).astype(jnp.bfloat16),
        axis=1,
    )
    outgoing = (
        lax.dot_general(
            send_map, expert_input, (((0,), (0,)), ((), ())), preferred_element_type=jnp.float32
        )
        .astype(jnp.bfloat16)
        .reshape(capacity, groups, model_width)
    )
    cells = capacity * EXPERTS
    combine_map = jnp.sum(
        jnp.where(
            (slots * EXPERTS + expert_index)[:, :, None] == jnp.arange(cells, dtype=jnp.int32),
            gate_values[:, :, None],
            0.0,
        ),
        axis=1,
    )
    piece_width = expert_first.shape[2] // local_experts
    first_local = expert_first.reshape(2, model_width, local_experts, piece_width)
    second_local = expert_second.reshape(local_experts, piece_width, model_width)
    arrived = lax.all_to_all(outgoing, ("seq", "head"), split_axis=1, concat_axis=1, tiled=True)
    slot_count = arrived.shape[0]
    grouped = arrived.reshape(slot_count, devices, local_experts, model_width)
    paired = jnp.einsum(
        "ksed,gdef->gksef", grouped, first_local, preferred_element_type=jnp.float32
    )
    hidden = (jax.nn.silu(paired[0]) * paired[1]).astype(jnp.bfloat16)
    produced = jnp.einsum(
        "ksef,efd->ksed", hidden, second_local, preferred_element_type=jnp.float32
    ).astype(jnp.bfloat16)
    returned = lax.all_to_all(
        produced.reshape(slot_count, devices * local_experts, model_width),
        ("seq", "head"),
        split_axis=1,
        concat_axis=1,
        tiled=True,
    )
    summed = jnp.sum(
        returned.reshape(capacity, EXPERTS, piece_count, model_width).astype(jnp.float32), axis=2
    )
    expert_sum = jnp.dot(
        combine_map, summed.reshape(cells, model_width), precision=lax.Precision.HIGHEST
    )
    return (residual + expert_sum).astype(jnp.bfloat16)


def solution(mesh):
    in_specs = (
        P("seq", None),
        P(),
        P(None, None, "head"),
        P(None, "head"),
        P("head", None),
        P(),
        P(),
        P(("seq", "head"), None),
        P(None, None, ("seq", "head")),
        P(("seq", "head"), None),
    )
    out_specs = P(("seq", "head"), None)
    return jax.shard_map(body, mesh=mesh, in_specs=in_specs, out_specs=out_specs, check_vma=False)
```

```python
import functools
import math

import jax
import jax.numpy as jnp
from jax import lax
from jax.experimental import pallas as pl
from jax.experimental.pallas import tpu as pltpu
from jax.sharding import PartitionSpec as P

HD = 128
EXPERTS = 64
TOP = 8


def partner_2(array, axis, apart):
    return lax.ppermute(array, axis, [(i, i ^ 1 << apart) for i in range(lax.axis_size(axis))])


def norm_scaled(values, gain):
    return values * lax.rsqrt(jnp.mean(values * values, axis=-1, keepdims=True) + 1e-06) * gain


def carried_kernel(breadth, heads, width, q_ref, memory_ref, out_ref, slab_ref):
    group = 16
    tokens = q_ref.shape[1]
    part = min(256, tokens)
    out_ref[...] = jnp.zeros_like(out_ref)
    place = lax.broadcasted_iota(jnp.int32, (breadth, heads * width), 0)

    def step(a, carry):
        for b in range(group):
            i = a * group + b
            fixed = (breadth - 1) * b - b * (b - 1) // 2
            shift = fixed % 8
            base = (
                a * (group * (breadth - 1) + group // 2)
                - a * a * (group * group // 2)
                - a * (group * b)
                + (fixed - shift)
            )
            rows = breadth + 8 if shift else breadth
            slab = memory_ref[pl.ds(pl.multiple_of(base, 8), rows), :]
            slab = slab[shift : shift + breadth]
            factor = jnp.where(place > i, math.sqrt(2.0), jnp.where(place == i, 1.0, 0.0))
            slab_ref[b] = (slab * factor).T.astype(jnp.bfloat16)
        for head in range(heads):
            q_rows = q_ref[pl.ds(pl.multiple_of(head * breadth + a * group, group), group), :]
            for first in range(0, tokens, part):
                columns = slice(first, first + part)
                weights = q_ref[head * breadth : (head + 1) * breadth, columns].astype(jnp.bfloat16)
                total = out_ref[head * width : (head + 1) * width, columns]
                for b in range(group):
                    inner = jnp.dot(
                        slab_ref[b, head * width : (head + 1) * width, :],
                        weights,
                        preferred_element_type=jnp.float32,
                    )
                    total = total + inner * q_rows[b : b + 1, columns]
                out_ref[head * width : (head + 1) * width, columns] = total
        return carry

    lax.fori_loop(0, breadth // group, step, 0)


def apply_carried(q_t, memory, heads, width):
    tokens = q_t.shape[1]
    return pl.pallas_call(
        functools.partial(carried_kernel, HD, heads, width),
        out_shape=jax.ShapeDtypeStruct((heads * width, tokens), jnp.float32),
        in_specs=[pl.BlockSpec(memory_space=pltpu.VMEM)] * 2,
        out_specs=pl.BlockSpec(memory_space=pltpu.VMEM),
        scratch_shapes=[pltpu.VMEM((16, heads * width, HD), jnp.bfloat16)],
        compiler_params=pltpu.CompilerParams(vmem_limit_bytes=40 * 2**20),
        cost_estimate=pl.CostEstimate(
            flops=4 * heads * width * HD * HD * tokens,
            bytes_accessed=memory.size * 4,
            transcendentals=0,
        ),
        name="carried_state",
    )(q_t, memory)


def causal_kernel(heads, width, me_ref, q_ref, keys_ref, values_ref, carried_ref, out_ref):
    shards, rows, _ = keys_ref.shape
    tokens = q_ref.shape[1]
    mine = me_ref[0]
    key_place = lax.broadcasted_iota(jnp.int32, (rows, tokens), 0)
    query_place = lax.broadcasted_iota(jnp.int32, (rows, tokens), 1) + mine * rows
    out_ref[...] = carried_ref[...]

    def shard_step(shard, carry):
        visible = key_place + shard * rows <= query_place
        for head in range(heads):
            scores = jnp.dot(
                keys_ref[shard, :, head * HD : (head + 1) * HD],
                q_ref[head * HD : (head + 1) * HD, :].astype(jnp.bfloat16),
                preferred_element_type=jnp.float32,
            )
            weights = jnp.where(visible, scores * scores, 0.0).astype(jnp.bfloat16)
            out_ref[head * width : (head + 1) * width, :] += lax.dot_general(
                values_ref[shard, :, head * width : (head + 1) * width],
                weights,
                (((0,), (0,)), ((), ())),
                preferred_element_type=jnp.float32,
            )
        return carry

    lax.fori_loop(0, mine + 1, shard_step, 0)


def causal_rows(q_t, keys, values, carried, heads, width):
    return pl.pallas_call(
        functools.partial(causal_kernel, heads, width),
        out_shape=jax.ShapeDtypeStruct(carried.shape, jnp.float32),
        in_specs=[pl.BlockSpec(memory_space=pltpu.SMEM)]
        + [pl.BlockSpec(memory_space=pltpu.VMEM)] * 4,
        out_specs=pl.BlockSpec(memory_space=pltpu.VMEM),
        compiler_params=pltpu.CompilerParams(vmem_limit_bytes=40 * 2**20),
        name="causal_scores",
    )(lax.axis_index("seq").astype(jnp.int32).reshape(1), q_t, keys, values, carried)


MESH = pl.DeviceIdType.MESH


def flipped(index, mask):
    bit = 1
    while bit <= mask:
        if mask & bit:
            index = index + bit - 2 * bit * ((index // bit) % 2)
        bit *= 2
    return index


def where_am_i():
    shard, head = lax.axis_index("seq"), lax.axis_index("head")
    return shard, head // 2, head % 2


def greet(devices):
    barrier = pltpu.get_barrier_semaphore()
    for device in devices:
        pl.semaphore_signal(barrier, inc=1, device_id=device, device_id_type=MESH)
    pl.semaphore_wait(barrier, len(devices))


def partners(shard, level, core, levels):
    sibling = (shard, level * 2 + 1 - core)
    across = [(flipped(shard, d), level * 2 + core) for d in (1, 2)]
    along = [(shard, flipped(level, k) * 2 + core) for k in range(1, levels)]
    return sibling, across, along


def spread_kernel(levels, own_ref, all_ref, own_sem, z_send, xy_send, diag_send, twin_send, recv):
    shard, level, core = where_am_i()
    sibling, across, along = partners(shard, level, core, levels)
    greet([sibling] + across + along)

    def place(d, k, other):
        mine = 1 - core if other else core
        return flipped(shard, d) * (2 * levels) + flipped(level, k) * 2 + mine

    keep = pltpu.make_async_copy(own_ref, all_ref.at[place(0, 0, 0)], own_sem)
    keep.start()
    started = []

    def push(d, k, send_sem, recv_sem, device):
        source = own_ref if d == 0 and k == 0 else all_ref.at[place(d, k, 0)]
        copy = pltpu.make_async_remote_copy(
            src_ref=source,
            dst_ref=all_ref.at[place(d, k, 0)],
            send_sem=send_sem,
            recv_sem=recv_sem,
            device_id=device,
            device_id_type=MESH,
        )
        copy.start()
        started.append(copy)

    def arrive(d, k, other):
        pltpu.make_async_remote_copy(
            src_ref=own_ref,
            dst_ref=all_ref.at[place(d, k, other)],
            send_sem=z_send.at[0],
            recv_sem=recv.at[d, k, other],
            device_id=sibling,
            device_id_type=MESH,
        ).wait_recv()

    for k in range(levels):
        if k > 0:
            arrive(0, k, 0)
        push(0, k, xy_send.at[0, k], recv.at[1, k, 0], across[0])
        push(0, k, xy_send.at[1, k], recv.at[2, k, 0], across[1])
        if k == 0:
            for far in range(1, levels):
                push(0, 0, z_send.at[far], recv.at[0, far, 0], along[far - 1])
        push(0, k, twin_send.at[0, k], recv.at[0, k, 1], sibling)
    for k in range(levels):
        for d in (1, 2):
            arrive(d, k, 0)
            if (k < levels // 2) == (d == 1):
                push(d, k, diag_send.at[k], recv.at[3, k, 0], across[2 - d])
            push(d, k, twin_send.at[d, k], recv.at[d, k, 1], sibling)
    for k in range(levels):
        arrive(3, k, 0)
        push(3, k, twin_send.at[3, k], recv.at[3, k, 1], sibling)
    for d in range(4):
        for k in range(levels):
            arrive(d, k, 1)
    for copy in started:
        copy.wait_send()
    keep.wait()


def spread(slab):
    levels = lax.axis_size("head") // 2
    dma = pltpu.SemaphoreType.DMA
    return pl.pallas_call(
        functools.partial(spread_kernel, levels),
        out_shape=jax.ShapeDtypeStruct((8 * levels,) + slab.shape, slab.dtype),
        in_specs=[pl.BlockSpec(memory_space=pl.ANY)],
        out_specs=pl.BlockSpec(memory_space=pl.ANY),
        scratch_shapes=[
            dma,
            dma((levels,)),
            dma((2, levels)),
            dma((levels,)),
            dma((4, levels)),
            dma((4, levels, 2)),
        ],
        compiler_params=pltpu.CompilerParams(collective_id=1, has_side_effects=True),
        name="spread_tokens",
    )(slab)


def collect_kernel(
    levels, part_ref, sum_ref, twin, diag, cross, line,
    twin_send, diag_send, cross_send, line_send, twin_recv, diag_recv, cross_recv, line_recv,
):
    shard, level, core = where_am_i()
    sibling, across, along = partners(shard, level, core, levels)
    greet([sibling] + across + along)
    started = []

    def place(d, k, other):
        mine = 1 - core if other else core
        return flipped(shard, d) * (2 * levels) + flipped(level, k) * 2 + mine

    def copy_of(source, target, send_sem, recv_sem, device):
        return pltpu.make_async_remote_copy(
            src_ref=source,
            dst_ref=target,
            send_sem=send_sem,
            recv_sem=recv_sem,
            device_id=device,
            device_id_type=MESH,
        )

    def push(*args):
        copy = copy_of(*args)
        copy.start()
        started.append(copy)

    def arrive(target, recv_sem):
        copy_of(target, target, twin_send.at[0, 0], recv_sem, sibling).wait_recv()

    def paired(d, k):
        arrive(twin.at[d, k], twin_recv.at[d, k])
        return part_ref[place(d, k, 0)].astype(jnp.float32) + twin[d, k].astype(jnp.float32)

    for d in (3, 1, 2, 0):
        for k in reversed(range(levels)):
            push(
                part_ref.at[place(d, k, 1)], twin.at[d, k],
                twin_send.at[d, k], twin_recv.at[d, k], sibling,
            )
    for k in reversed(range(levels)):
        twin[3, k] = paired(3, k).astype(twin.dtype)
        push(
            twin.at[3, k], diag.at[k], diag_send.at[k], diag_recv.at[k],
            across[0 if k < levels // 2 else 1],
        )
    for relayed in (False, True):
        for k in reversed(range(levels)):
            for d in (1, 2):
                if ((k < levels // 2) == (d == 2)) != relayed:
                    continue
                value = paired(d, k)
                if relayed:
                    arrive(diag.at[k], diag_recv.at[k])
                    value = value + diag[k].astype(jnp.float32)
                twin[d, k] = value.astype(twin.dtype)
                push(
                    twin.at[d, k], cross.at[d - 1, k],
                    cross_send.at[d - 1, k], cross_recv.at[d - 1, k], across[d - 1],
                )
    for k in reversed(range(levels)):
        value = paired(0, k)
        for side in (0, 1):
            arrive(cross.at[side, k], cross_recv.at[side, k])
            value = value + cross[side, k].astype(jnp.float32)
        if k > 0:
            twin[0, k] = value.astype(twin.dtype)
            push(twin.at[0, k], line.at[k], line_send.at[k], line_recv.at[k], along[k - 1])
        else:
            sum_ref[...] = value
    for k in range(1, levels):
        arrive(line.at[k], line_recv.at[k])
        sum_ref[...] += line[k].astype(jnp.float32)
    for copy in started:
        copy.wait_send()


def collect(parts):
    levels = lax.axis_size("head") // 2
    dma = pltpu.SemaphoreType.DMA
    slab = parts.shape[1:]
    counts = [(4, levels), (levels,), (2, levels), (levels,)]
    return pl.pallas_call(
        functools.partial(collect_kernel, levels),
        out_shape=jax.ShapeDtypeStruct(slab, jnp.float32),
        in_specs=[pl.BlockSpec(memory_space=pltpu.VMEM)],
        out_specs=pl.BlockSpec(memory_space=pltpu.VMEM),
        scratch_shapes=[pltpu.VMEM(count + slab, parts.dtype) for count in counts]
        + [dma(count) for count in counts] * 2,
        compiler_params=pltpu.CompilerParams(
            collective_id=2, has_side_effects=True, vmem_limit_bytes=40 * 2**20
        ),
        name="collect_sums",
    )(parts)


def expert_kernel(
    groups, rows, span, code_rows_ref, code_ref, high_ref, low_ref, tokens_ref,
    first_ref, second_ref, out_ref, chosen, total,
):
    expert, step = pl.program_id(0), pl.program_id(1)
    width = out_ref.shape[1]

    @pl.when(step == 0)
    def _():
        slot = lax.broadcasted_iota(jnp.int32, (rows, span), 0)
        for g in range(groups):
            select = jnp.where(slot == code_rows_ref[0, g : g + 1, :], 1.0, 0.0).astype(jnp.bfloat16)
            chosen[g * rows : (g + 1) * rows, :] = jnp.dot(
                select,
                tokens_ref[g * span : (g + 1) * span, :width],
                preferred_element_type=jnp.float32,
            ).astype(jnp.bfloat16)
        total[...] = jnp.zeros_like(total)

    inputs = chosen[...]
    gate_part = jnp.dot(inputs, first_ref[0], preferred_element_type=jnp.float32)
    up_part = jnp.dot(inputs, first_ref[1], preferred_element_type=jnp.float32)
    hidden = (gate_part / (1.0 + jnp.exp(-gate_part)) * up_part).astype(jnp.bfloat16)
    total[...] += jnp.dot(hidden, second_ref[...], preferred_element_type=jnp.float32)

    @pl.when(step == pl.num_programs(1) - 1)
    def _():
        slot = lax.broadcasted_iota(jnp.int32, (span, rows), 1)
        for g in range(groups):
            tokens = slice(g * span, (g + 1) * span)
            produced = total[g * rows : (g + 1) * rows, :].astype(jnp.bfloat16)
            hit = slot == code_ref[0, tokens, :]
            mixed = jnp.dot(
                jnp.where(hit, high_ref[0, tokens, :], 0.0).astype(jnp.bfloat16),
                produced,
                preferred_element_type=jnp.float32,
            ) + jnp.dot(
                jnp.where(hit, low_ref[0, tokens, :], 0.0).astype(jnp.bfloat16),
                produced,
                preferred_element_type=jnp.float32,
            )

            @pl.when(expert == 0)
            def _():
                out_ref[tokens, :] = mixed.astype(out_ref.dtype)

            @pl.when(expert > 0)
            def _():
                out_ref[tokens, :] = (out_ref[tokens, :].astype(jnp.float32) + mixed).astype(
                    out_ref.dtype
                )


def run_experts(code, high, low, rows, span, tokens, expert_first, expert_second):
    local_experts, count = code.shape
    width = expert_second.shape[1]
    piece = expert_second.shape[0] // local_experts
    chunk = min(256, piece)
    steps = piece // chunk
    groups = count // span
    whole = dict(pipeline_mode=pl.Buffered(1))
    column = pl.BlockSpec((1, count, 1), lambda e, f: (e, 0, 0), **whole)
    return pl.pallas_call(
        functools.partial(expert_kernel, groups, rows, span),
        grid=(local_experts, steps),
        out_shape=jax.ShapeDtypeStruct((count, width), jnp.bfloat16),
        in_specs=[
            pl.BlockSpec((1, groups, span), lambda e, f: (e, 0, 0)),
            column,
            column,
            column,
            pl.BlockSpec(tokens.shape, lambda e, f: (0, 0), **whole),
            pl.BlockSpec((2, width, chunk), lambda e, f: (0, 0, e * steps + f)),
            pl.BlockSpec((chunk, width), lambda e, f: (e * steps + f, 0)),
        ],
        out_specs=pl.BlockSpec((count, width), lambda e, f: (0, 0), **whole),
        scratch_shapes=[
            pltpu.VMEM((groups * rows, width), jnp.bfloat16),
            pltpu.VMEM((groups * rows, width), jnp.float32),
        ],
        compiler_params=pltpu.CompilerParams(vmem_limit_bytes=52 * 2**20),
        name="experts",
    )(
        code.reshape(local_experts, groups, span),
        code[:, :, None],
        high[:, :, None],
        low[:, :, None],
        tokens,
        expert_first,
        expert_second,
    )


def body(
    tokens,
    attention_gain,
    head_weights,
    carried_state,
    output_weight,
    expert_gain,
    router_weight,
    expert_index,
    expert_first,
    expert_second,
):
    shard_rows = tokens.shape[0]
    model_width = tokens.shape[1]
    floats = tokens.astype(jnp.float32)
    normed = norm_scaled(floats, attention_gain).astype(jnp.bfloat16)
    projected = jnp.einsum(
        "td,adc->atc", normed, head_weights, preferred_element_type=jnp.float32
    ).astype(jnp.bfloat16)
    query_rows, key_rows, value_rows = (projected[0], projected[1], projected[2])
    share = value_rows.shape[1]
    local_heads = max(1, share // HD)
    value_width = share // local_heads
    if value_width < HD:
        mine = jnp.stack([query_rows, key_rows])
        partner = partner_2(mine, "head", 0)
        lower = lax.axis_index("head") % 2 == 0
        joined = jnp.where(
            lower,
            jnp.concatenate([mine, partner], axis=2),
            jnp.concatenate([partner, mine], axis=2),
        )
        query_rows, key_rows = (joined[0], joined[1])

    gathered = lax.all_gather(jnp.concatenate([key_rows, value_rows], axis=1), "seq")
    key_width = key_rows.shape[1]
    q_t = query_rows.T.astype(jnp.float32)
    carried = apply_carried(q_t, carried_state, local_heads, value_width)
    raw_t = causal_rows(
        q_t,
        gathered[:, :, :key_width],
        gathered[:, :, key_width:],
        carried,
        local_heads,
        value_width,
    ).reshape(local_heads, value_width, shard_rows) / HD
    squares = jnp.sum(raw_t * raw_t, axis=1, keepdims=True)
    if value_width < HD:
        squares = squares + partner_2(squares, "head", 0)
    scaled_heads = (raw_t * lax.rsqrt(squares / HD + 1e-06)).astype(jnp.bfloat16)
    attended = scaled_heads.reshape(share, shard_rows).T
    slab_rows = expert_index.shape[0]
    attention_sum = lax.psum_scatter(
        jnp.dot(attended, output_weight, preferred_element_type=jnp.float32).astype(jnp.bfloat16),
        "head",
        scatter_dimension=0,
        tiled=True,
    ).astype(jnp.float32)
    token_slab = lax.dynamic_slice_in_dim(floats, lax.axis_index("head") * slab_rows, slab_rows, 0)
    residual = token_slab + attention_sum
    expert_input = norm_scaled(residual, expert_gain).astype(jnp.bfloat16)
    logits = jnp.dot(expert_input, router_weight, preferred_element_type=jnp.float32)
    matches = expert_index[:, :, None] == jnp.arange(EXPERTS, dtype=jnp.int32)
    gate_values = jax.nn.sigmoid(jnp.sum(jnp.where(matches, logits[:, None, :], 0.0), axis=2))
    dense = jnp.sum(jnp.where(matches, gate_values[:, :, None], 0.0), axis=1)
    dense_high = dense.astype(jnp.bfloat16)
    dense_low = (dense - dense_high.astype(jnp.float32)).astype(jnp.bfloat16)
    everyone = spread(jnp.concatenate([expert_input, dense_high, dense_low], axis=1))
    devices = lax.axis_size("seq") * lax.axis_size("head")
    local_experts = max(1, EXPERTS // devices)
    capacity = max(2, 3 * slab_rows * TOP // (2 * EXPERTS))
    slabs = max(1, 256 // slab_rows)
    count = devices * slab_rows
    position = lax.axis_index("seq") * lax.axis_size("head") + lax.axis_index("head")
    mine = position * EXPERTS // devices + jnp.arange(local_experts, dtype=jnp.int32)
    picks = (jnp.arange(EXPERTS, dtype=jnp.int32)[:, None] == mine).astype(jnp.bfloat16)
    flat = everyone.reshape(count, -1)

    def own_gates(first):
        return lax.dot_general(
            picks,
            flat[:, first : first + EXPERTS],
            (((0,), (1,)), ((), ())),
            preferred_element_type=jnp.float32,
        )

    high, low = own_gates(model_width), own_gates(model_width + EXPERTS)
    named = (high != 0.0).reshape(local_experts, devices, slab_rows)
    before = jnp.tril(jnp.ones((slab_rows, slab_rows), jnp.bfloat16), -1)
    rank = jnp.einsum(
        "edt,ut->edu", named.astype(jnp.bfloat16), before, preferred_element_type=jnp.float32
    ).astype(jnp.int32)
    base = (jnp.arange(devices, dtype=jnp.int32) % slabs * capacity)[None, :, None]
    code = jnp.where(named, base + rank, -1).reshape(local_experts, count)
    parts = run_experts(
        code, high, low, slabs * capacity, slabs * slab_rows, flat, expert_first, expert_second
    )
    expert_sum = collect(parts.reshape(devices, slab_rows, model_width))
    return (residual + expert_sum).astype(jnp.bfloat16)


def solution(mesh):
    in_specs = (
        P("seq", None),
        P(),
        P(None, None, "head"),
        P(None, "head"),
        P("head", None),
        P(),
        P(),
        P(("seq", "head"), None),
        P(None, None, ("seq", "head")),
        P(("seq", "head"), None),
    )
    out_specs = P(("seq", "head"), None)
    return jax.shard_map(body, mesh=mesh, in_specs=in_specs, out_specs=out_specs, check_vma=False)
```
